32 devices in a mesh: ep: 16 (over z, x, core), tp: 2 (over y).
Axes of the slice: x: 2, y: 2, z: 4, core: 2. Of those that a mesh axis runs over, the one named last changes fastest.
Arguments:
- tokens: bfloat16 [256, 7168], P('ep', 'tp'), may hold values from -6 to 6
- expert_ids: int32 [256, 8], P('ep'), may hold values from 0 to 15, all different within a row; in each aligned block of 16 rows (0 to 15, 16 to 31, ...) at most 16 rows name the same one
- gate_weights: float32 [256, 8], P('ep'), may hold values from 0.05 to 0.6
- w_gate: bfloat16 [16, 7168, 2048], P('ep', None, 'tp'), may hold values from -0.0625 to 0.0625
- w_up: bfloat16 [16, 7168, 2048], P('ep', None, 'tp'), may hold values from -0.0625 to 0.0625
- w_down: bfloat16 [16, 2048, 7168], P('ep', None, 'tp'), may hold values from -0.125 to 0.125
Outputs:
- moe_out: bfloat16 [256, 7168], P('ep', 'tp')
The draws below stay inside these ranges and needn't reach their ends.
Inputs may be any that keep to these rules, and one draw needn't show every extreme that they name: `expert_ids`: each row names 8 different experts. Among the 16 rows of one index of ep (aligned blocks) no expert is named by more than 16 rows, a bound that some block reaches.
All inputs are finite; a program needn't handle non-finite values.
Results may differ from the reference program's by a relative error of at most 0.012.
Values may be sent and summed in bfloat16 or wider, within the bound.
A program may use at most 128 MiB of HBM per device.

```python
import math
import jax
import jax.numpy as jnp
import numpy as np
from jax import lax

D = 7168
FF = 2048
TOP = 8
CAP = 16
TOK_GRP = 16
TOKENS = 256
EXPERTS = 16
N_EP = 16


def steps_of(stream_key, extent, shards, smallest, high):
    def one(axis_at, shards_of):
        heights = jax.random.uniform(jax.random.fold_in(jax.random.fold_in(stream_key, 6), axis_at), (shards_of,), jnp.float32, smallest / len(shards), high / len(shards))
        return jnp.repeat(jnp.exp(heights), extent[axis_at] // shards_of).reshape((-1,) + (1,) * (len(extent) - axis_at - 1))

    level = one(*shards[0])
    for cut in shards[1:]:
        level = level * one(*cut)
    return level


def deal_out(own_key, own, number, rows, number_of, top, most, skew):
    order = jax.random.permutation(own_key, number_of)
    packed, usual = portions_of(number_of, rows * top, most, skew, True), portions_of(number_of, rows * top, most, skew, False)
    places = jnp.arange(number_of)

    def named(sizes, offset_by):
        used = int((sizes > 0).sum())
        fixed = max(1, used // 4)
        moved = fixed + (places - fixed + offset_by * (used - fixed)) % max(1, number_of - fixed)
        return jnp.zeros((number_of,), jnp.int32).at[order[jnp.where(places < fixed, places, moved)]].set(jnp.asarray(sizes, jnp.int32))

    sizes = jnp.where(number % 4 == 0, named(packed, number // 4), named(usual, number - number // 4 - 1))
    mixed = jax.random.permutation(jax.random.fold_in(own, 3), number_of)
    donor, receiver = mixed[0:number_of // 2 * 2:2], mixed[1:number_of // 2 * 2:2]
    room = jnp.minimum(sizes[donor] - 1, most - sizes[receiver]) // 2
    room = jnp.where((donor == order[0]) | (receiver == order[0]) | (sizes[receiver] == 0), 0, jnp.maximum(room, 0))
    moved = jax.random.randint(jax.random.fold_in(own, 4), (number_of // 2,), 0, 1 << 20) % (room + 1)
    sizes = sizes.at[donor].add(-moved).at[receiver].add(moved)
    labels = jnp.searchsorted(jnp.cumsum(sizes), jnp.arange(rows * top), side="right").astype(jnp.int32)
    listing = labels.reshape(top, rows).T
    listing = listing[jax.random.permutation(jax.random.fold_in(own, 1), rows)]
    offset_by = jax.random.randint(jax.random.fold_in(own, 2), (rows, 1), 0, top)
    return jnp.take_along_axis(listing, (jnp.arange(top)[None, :] + offset_by) % top, axis=1)


def portions_of(amount, total, bound, skew, full):
    portions = [(1 << 20) // math.isqrt(grade ** skew) + 1 for grade in range(1, amount + 1)]
    largest = bound if full else min(bound, max(-(-total // amount), total * portions[0] // sum(portions)))
    least = 1 if total - largest >= amount - 1 else 0
    holding, rest = [largest] + [least] * (amount - 1), total - largest - least * (amount - 1)
    while rest > 0:
        movable = [i for i in range(1, amount) if holding[i] < largest] or [i for i in range(1, amount) if holding[i] < bound]
        whole, left = sum([portions[i] for i in movable]), rest
        for i in movable:
            extra = min(bound - holding[i], max(1, left * portions[i] // whole), rest)
            holding[i] = holding[i] + extra
            rest = rest - extra
    return np.array(holding)


def centred(stream_key, extent, deviation, most, cuts=(), kind=jnp.bfloat16):
    gain = steps_of(stream_key, extent, cuts, -0.22, 0.18) if cuts else 1.0
    values = jax.random.normal(stream_key, extent, jnp.float32) * deviation * gain
    return jnp.minimum(jnp.maximum(values, -most), most).astype(kind)


def setup_inputs(seed: int = 0) -> dict:
    streams_of = jax.random.split(jax.random.key(seed), 7)
    tokens = centred(streams_of[0], (TOKENS, D), 1.0, 6.0, ((0, 16), (1, 2)))
    expert_ids_keys = jax.random.split(jax.random.fold_in(streams_of[1], 1), TOKENS // TOK_GRP)
    expert_ids_turns = jax.random.permutation(jax.random.fold_in(streams_of[1], 3), TOKENS // TOK_GRP)
    expert_ids = jax.vmap(lambda own, number: deal_out(jax.random.fold_in(streams_of[1], 2), own, number, TOK_GRP, EXPERTS, TOP, CAP, 2))(expert_ids_keys, expert_ids_turns).reshape((TOKENS, TOP))
    gate_weights = jnp.clip(0.05 + 0.55 * jax.random.uniform(streams_of[2], (TOKENS, TOP), jnp.float32) ** steps_of(streams_of[2], (TOKENS, TOP), ((0, 16),), -0.2, 0.2), 0.05, 0.6)
    w_gate = centred(streams_of[3], (EXPERTS, D, FF), D ** -0.5, 0.0625, ((0, 16), (2, 2)))
    w_up = centred(streams_of[4], (EXPERTS, D, FF), D ** -0.5, 0.0625, ((0, 16), (2, 2)))
    w_down = centred(streams_of[5], (EXPERTS, FF, D), FF ** -0.5, 0.125, ((0, 16), (2, 2)))
    return dict(tokens=tokens, expert_ids=expert_ids, gate_weights=gate_weights, w_gate=w_gate, w_up=w_up, w_down=w_down)


def slot_index(group_ids):
    flat_ids = group_ids.reshape(-1)
    onehot = (flat_ids[:, None] == jnp.arange(EXPERTS, dtype=jnp.int32)[None, :]).astype(jnp.int32)
    before = jnp.cumsum(onehot, axis=0) - onehot
    position = jnp.sum(before * onehot, axis=1)
    return (flat_ids * CAP + position).astype(jnp.int32)


def expert_apply(operands):
    in_rows, gate_mat, up_mat, down_mat = operands
    gate_sum = jnp.dot(in_rows, gate_mat, preferred_element_type=jnp.float32)
    up_sum = jnp.dot(in_rows, up_mat, preferred_element_type=jnp.float32)
    hidden = (jax.nn.silu(gate_sum) * up_sum).astype(jnp.bfloat16)
    return jnp.dot(hidden, down_mat, preferred_element_type=jnp.float32).astype(jnp.bfloat16)


def reference(tokens, expert_ids, gate_weights, w_gate, w_up, w_down):
    group_ids = expert_ids.reshape(N_EP, TOK_GRP, TOP)
    slot_of = jax.vmap(slot_index)(group_ids)
    grouped = tokens.reshape(N_EP, TOK_GRP, D)
    copies = jnp.repeat(grouped, TOP, axis=1)
    buffer = jnp.zeros((N_EP, EXPERTS * CAP, D), jnp.bfloat16)
    buffer = jax.vmap(lambda held, where, rows_in: held.at[where].set(rows_in))(buffer, slot_of, copies)
    per_expert = buffer.reshape(N_EP, EXPERTS, CAP, D).transpose(1, 0, 2, 3).reshape(EXPERTS, N_EP * CAP, D)
    expert_out = lax.map(expert_apply, (per_expert, w_gate, w_up, w_down))
    returned = expert_out.reshape(EXPERTS, N_EP, CAP, D).transpose(1, 0, 2, 3).reshape(N_EP, EXPERTS * CAP, D)
    picked = jax.vmap(lambda held, where: held[where])(returned, slot_of).reshape(N_EP, TOK_GRP, TOP, D)
    weights = gate_weights.reshape(N_EP, TOK_GRP, TOP).astype(jnp.float32)
    mixed = jnp.einsum("sgk,sgkd->sgd", weights, picked.astype(jnp.float32))
    return mixed.reshape(TOKENS, D).astype(jnp.bfloat16)
```

```python
import jax
import jax.numpy as jnp
from jax import lax
from jax.sharding import PartitionSpec as P


def per_device(tokens, expert_ids, gate_weights, w_gate, w_up, w_down):
    n_experts = lax.axis_size("ep")
    experts = jnp.arange(n_experts, dtype=jnp.int32)
    chosen = expert_ids[:, :, None] == experts[None, None, :]
    share = jnp.sum(jnp.where(chosen, gate_weights[:, :, None], 0.0), axis=1)
    share = lax.all_gather(share, "ep", axis=0, tiled=True)
    mine = experts == lax.axis_index("ep")
    share = jnp.sum(jnp.where(mine[None, :], share, 0.0), axis=1, keepdims=True)
    rows = lax.all_gather(tokens, "tp", axis=1, tiled=True)
    rows = lax.all_gather(rows, "ep", axis=0, tiled=True)
    gate_sum = jnp.dot(rows, w_gate[0], preferred_element_type=jnp.float32)
    up_sum = jnp.dot(rows, w_up[0], preferred_element_type=jnp.float32)
    hidden = (jax.nn.silu(gate_sum) * up_sum).astype(jnp.bfloat16)
    hidden = lax.all_gather(hidden, "tp", axis=1, tiled=True)
    result = jnp.dot(hidden, w_down[0], preferred_element_type=jnp.float32)
    result = (result * share).astype(jnp.bfloat16)
    return lax.psum_scatter(result, "ep", scatter_dimension=0, tiled=True)


def solution(mesh):
    return jax.shard_map(
        per_device,
        mesh=mesh,
        in_specs=(
            P("ep", "tp"),
            P("ep", None),
            P("ep", None),
            P("ep", None, "tp"),
            P("ep", None, "tp"),
            P("ep", None, "tp"),
        ),
        out_specs=P("ep", "tp"),
        check_vma=False,
    )
```

```python
import functools

import jax
import jax.numpy as jnp
from jax import lax
from jax.experimental import pallas as pl
from jax.experimental.pallas import tpu as pltpu
from jax.sharding import PartitionSpec as P

MESH = pl.DeviceIdType.MESH
LANES = 128


def share_of(expert_ids, gate_weights, n_experts):
    experts = jnp.arange(n_experts, dtype=jnp.int32)
    chosen = expert_ids[:, :, None] == experts[None, None, :]
    return jnp.sum(jnp.where(chosen, gate_weights[:, :, None], 0.0), axis=1)


def plain(tokens, expert_ids, gate_weights, w_gate, w_up, w_down):
    n_experts = lax.axis_size("ep")
    share = share_of(expert_ids, gate_weights, n_experts)
    share = lax.all_gather(share, "ep", axis=0, tiled=True)
    mine = jnp.arange(n_experts, dtype=jnp.int32) == lax.axis_index("ep")
    share = jnp.sum(jnp.where(mine[None, :], share, 0.0), axis=1, keepdims=True)
    rows = lax.all_gather(tokens, "tp", axis=1, tiled=True)
    rows = lax.all_gather(rows, "ep", axis=0, tiled=True)
    gate_sum = jnp.dot(rows, w_gate[0], preferred_element_type=jnp.float32)
    up_sum = jnp.dot(rows, w_up[0], preferred_element_type=jnp.float32)
    hidden = (jax.nn.silu(gate_sum) * up_sum).astype(jnp.bfloat16)
    hidden = lax.all_gather(hidden, "tp", axis=1, tiled=True)
    result = jnp.dot(hidden, w_down[0], preferred_element_type=jnp.float32)
    result = (result * share).astype(jnp.bfloat16)
    return lax.psum_scatter(result, "ep", scatter_dimension=0, tiled=True)


def kernel(tok, shares, wg_hbm, wu_hbm, wd_hbm, out,
           x_buf, wg, wu, wd, hid, acc, part, r0, s0, r1, s1, r2, sh, col,
           w_sem, own_sem, own_s, own_r, sh_s, sh_r, z_s, z_r, s_s, s_r, t_s, t_r, b_s, b_r,
           h_s, h_r, q0_s, q0_r, q1_s, q1_r, q2_s, q2_r):
    e = lax.axis_index("ep")
    y = lax.axis_index("tp")
    z, x, c = e // 4, (e // 2) % 2, e % 2
    zh, zl = z // 2, z % 2
    wide = tok.shape[1] // 2
    n_q = part.shape[0]
    q_cols = part.shape[3]

    def at(z_, x_, c_, y_):
        return ((z_ * 2 + x_) * 2 + c_, y_)

    z_of = [z, zh * 2 + 1 - zl, (1 - zh) * 2 + zl, (1 - zh) * 2 + 1 - zl]
    sib = at(z, x, 1 - c, y)
    x_peer = at(z, 1 - x, c, y)
    y_peer = (e, 1 - y)
    sx, sy = x + (1 - c) * (1 - 2 * x), y + c * (1 - 2 * y)
    tx, ty = x + c * (1 - 2 * x), y + (1 - c) * (1 - 2 * y)
    s_peer, t_peer = at(z, sx, c, sy), at(z, tx, c, ty)

    def block(z_, x_, y_, c_):
        return x_buf.at[2 * y_ + c_, :, pl.ds(16 * (4 * x_ + z_), 16), :]

    def own_block(color, c_):
        return x_buf.at[2 * y + color, c_, pl.ds(16 * (4 * x + z), 16), :]

    def remote(src, dst, ss, rs, dev):
        return pltpu.make_async_remote_copy(
            src_ref=src, dst_ref=dst, send_sem=ss, recv_sem=rs, device_id=dev, device_id_type=MESH
        )

    loads = []
    for k in range(4):
        kb = pl.ds(k * wide, wide)
        loads.append(pltpu.make_async_copy(wg_hbm.at[0, kb, :], wg.at[k], w_sem.at[2 * k]))
        loads.append(pltpu.make_async_copy(wu_hbm.at[0, kb, :], wu.at[k], w_sem.at[2 * k + 1]))
    half = wd.shape[1]
    for k in range(2):
        loads.append(
            pltpu.make_async_copy(wd_hbm.at[0, pl.ds(k * half, half), :], wd.at[k], w_sem.at[8 + k])
        )

    barrier = pltpu.get_barrier_semaphore()
    for i in range(1, 16):
        pl.semaphore_signal(barrier, inc=1, device_id=((e + i) % 16, y), device_id_type=MESH)
    pl.semaphore_signal(barrier, inc=1, device_id=y_peer, device_id_type=MESH)
    own = [
        pltpu.make_async_copy(tok.at[:, pl.ds(k * wide, wide)], own_block(k, c), own_sem.at[k])
        for k in range(2)
    ]
    for cp in own:
        cp.start()
    for cp in loads:
        cp.start()
    pl.semaphore_wait(barrier, 16)

    sent = []

    def go(src, dst, ss, rs, dev):
        cp = remote(src, dst, ss, rs, dev)
        cp.start()
        sent.append(cp)

    for k in range(2):
        go(tok.at[:, pl.ds(k * wide, wide)], own_block(k, c), own_s.at[k], own_r.at[k], sib)

    own[0].wait()
    own[1].wait()
    for k in range(2):
        remote(own_block(k, 1 - c), own_block(k, 1 - c), own_s.at[k], own_r.at[k], sib).wait_recv()

    def same(ref, ss, rs, dev):
        go(ref, ref, ss, rs, dev)

    def got(ref, rs):
        remote(ref, ref, own_s.at[0], rs, sib).wait_recv()

    mine = block(z, x, y, c)
    same(mine, s_s.at[0], s_r.at[0], s_peer)
    same(mine, t_s.at[0], t_r.at[0], t_peer)
    for k in range(1, 4):
        same(mine, z_s.at[k - 1], z_r.at[k - 1], at(z_of[k], x, c, y))

    pos = (c * 2 + x) * 4 + z
    for i in range(1, 16):
        to = (e + i) % 16
        go(shares.at[to], sh.at[pos], sh_s.at[i - 1], sh_r.at[i - 1], (to, y))
    own_share = pltpu.make_async_copy(shares.at[e], sh.at[pos], own_sem.at[2])
    own_share.start()

    for k in range(1, 4):
        b = block(z_of[k], x, y, c)
        got(b, z_r.at[k - 1])
        same(b, s_s.at[k], s_r.at[k], s_peer)
        same(b, t_s.at[k], t_r.at[k], t_peer)
        same(b, b_s.at[k - 1], b_r.at[k - 1], sib)
    for k in range(4):
        b = block(z_of[k], sx, sy, c)
        got(b, s_r.at[k])
        same(b, t_s.at[4 + k], t_r.at[4 + k], t_peer)
        same(b, b_s.at[3 + k], b_r.at[3 + k], sib)
    for f in range(2):
        for k in range(4):
            fx = tx if f == 0 else 1 - x
            fy = ty if f == 0 else 1 - y
            b = block(z_of[k], fx, fy, c)
            got(b, t_r.at[4 * f + k])
            same(b, b_s.at[7 + 4 * f + k], b_r.at[7 + 4 * f + k], sib)

    own_share.wait()
    for i in range(1, 16):
        remote(sh.at[pos], sh.at[pos], sh_s.at[i - 1], sh_r.at[i - 1], sib).wait_recv()
    pick = lax.broadcasted_iota(jnp.int32, (16, LANES), 0) == lax.broadcasted_iota(
        jnp.int32, (16, LANES), 1
    )
    for p in range(16):
        row = jnp.where(pick, sh[p], 0.0)
        col[pl.ds(16 * p, 16), :] = jnp.sum(row, axis=1, keepdims=True)

    for i in range(15):
        got(mine, b_r.at[i])
    for cp in loads[:8]:
        cp.wait()

    rows = 256
    n_h = h_s.shape[0]
    h_cols = hid.shape[2] // n_h

    def hidden_copy(n):
        ref = hid.at[y, :, pl.ds(pl.multiple_of(n * h_cols, h_cols), h_cols)]
        return remote(ref, ref, h_s.at[n], h_r.at[n], y_peer)

    @pl.loop(0, n_h)
    def _(n):
        cols = pl.ds(pl.multiple_of(n * h_cols, h_cols), h_cols)
        g = jnp.zeros((rows, h_cols), jnp.float32)
        u = jnp.zeros((rows, h_cols), jnp.float32)
        for k in range(4):
            xk = x_buf[k].reshape(rows, wide)
            g = g + jnp.dot(xk, wg[k, :, cols], preferred_element_type=jnp.float32)
            u = u + jnp.dot(xk, wu[k, :, cols], preferred_element_type=jnp.float32)
        hid[y, :, cols] = (g / (1.0 + jnp.exp(-g)) * u).astype(jnp.bfloat16)
        hidden_copy(n).start()

    for cp in loads[8:]:
        cp.wait()

    @pl.loop(0, n_q)
    def _(q):
        cols = pl.ds(pl.multiple_of(q * q_cols, q_cols), q_cols)
        acc[:, cols] = jnp.dot(hid[y], wd[y, :, cols], preferred_element_type=jnp.float32)

    for n in range(n_h):
        hidden_copy(n).wait()

    def r0_copy(q):
        return remote(part.at[q, 1 - c], r0.at[q], q0_s.at[q], q0_r.at[q], sib)

    def r1_copy(q):
        src = s0.at[q, pl.ds(64 * (1 - x), 64), :]
        return remote(src, r1.at[q], q1_s.at[q], q1_r.at[q], x_peer)

    def r2_copy(q, k):
        src = s1.at[q, pl.ds(16 * z_of[k], 16), :]
        return remote(
            src, r2.at[q, k - 1], q2_s.at[3 * q + k - 1], q2_r.at[3 * q + k - 1], at(z_of[k], x, c, y)
        )

    f32 = jnp.float32

    @pl.loop(0, n_q + 3)
    def _(i):
        @pl.when(i < n_q)
        def _():
            cols = pl.ds(pl.multiple_of(i * q_cols, q_cols), q_cols)
            r = acc[:, cols] + jnp.dot(hid[1 - y], wd[1 - y, :, cols], preferred_element_type=f32)
            part[i] = (r * col[...]).astype(jnp.bfloat16).reshape(2, rows // 2, q_cols)
            r0_copy(i).start()

        @pl.when((i >= 1) & (i < n_q + 1))
        def _():
            q = i - 1
            r0_copy(q).wait()
            s0[q] = (part[q, c].astype(f32) + r0[q].astype(f32)).astype(jnp.bfloat16)
            r1_copy(q).start()

        @pl.when((i >= 2) & (i < n_q + 2))
        def _():
            q = i - 2
            r1_copy(q).wait()
            keep = s0[q, pl.ds(pl.multiple_of(64 * x, 64), 64), :].astype(f32)
            s1[q] = (keep + r1[q].astype(f32)).astype(jnp.bfloat16)
            for k in range(1, 4):
                r2_copy(q, k).start()

        @pl.when(i >= 3)
        def _():
            q = i - 3
            total = s1[q, pl.ds(pl.multiple_of(16 * z, 16), 16), :].astype(f32)
            for k in range(1, 4):
                r2_copy(q, k).wait()
                total = total + r2[q, k - 1].astype(f32)
            out[:, pl.ds(pl.multiple_of(q * q_cols, q_cols), q_cols)] = total.astype(jnp.bfloat16)

    for cp in sent:
        cp.wait_send()


def fused(tokens, expert_ids, gate_weights, w_gate, w_up, w_down):
    bf16, f32 = jnp.bfloat16, jnp.float32
    width = tokens.shape[1]
    depth, units = w_gate.shape[1], w_gate.shape[2]
    share = share_of(expert_ids, gate_weights, 16).T
    share = jnp.pad(share, ((0, 0), (0, LANES - 16)))[:, None, :]
    n_q, n_h = 7, 4
    q_cols = width // n_q
    wide = width // 2
    vmem, dma = pltpu.VMEM, pltpu.SemaphoreType.DMA
    hbm = pl.BlockSpec(memory_space=pl.ANY)
    return pl.pallas_call(
        kernel,
        out_shape=jax.ShapeDtypeStruct((16, width), bf16),
        in_specs=[hbm] * 5,
        out_specs=pl.BlockSpec(memory_space=pltpu.VMEM),
        scratch_shapes=[
            vmem((4, 2, 128, wide), bf16),
            vmem((4, wide, units), bf16),
            vmem((4, wide, units), bf16),
            vmem((2, units, width), bf16),
            vmem((2, 256, units), bf16),
            vmem((256, width), f32),
            vmem((n_q, 2, 128, q_cols), bf16),
            vmem((n_q, 128, q_cols), bf16),
            vmem((n_q, 128, q_cols), bf16),
            vmem((n_q, 64, q_cols), bf16),
            vmem((n_q, 64, q_cols), bf16),
            vmem((n_q, 3, 16, q_cols), bf16),
            vmem((16, 1, LANES), f32),
            vmem((256, 1), f32),
            dma((10,)), dma((3,)), dma((2,)), dma((2,)), dma((15,)), dma((15,)),
            dma((3,)), dma((3,)), dma((4,)), dma((4,)), dma((8,)), dma((8,)), dma((15,)), dma((15,)),
            dma((n_h,)), dma((n_h,)),
            dma((n_q,)), dma((n_q,)), dma((n_q,)), dma((n_q,)), dma((3 * n_q,)), dma((3 * n_q,)),
        ],
        compiler_params=pltpu.CompilerParams(
            collective_id=0, has_side_effects=True, vmem_limit_bytes=62_000_000
        ),
        cost_estimate=pl.CostEstimate(
            flops=2 * 256 * (depth * units * 2 + 2 * units * width),
            bytes_accessed=2 * (2 * depth * units + 2 * units * width),
            transcendentals=256 * units,
        ),
    )(tokens, share, w_gate, w_up, w_down)


def solution(mesh):
    one_kernel = mesh.shape["ep"] == 16 and mesh.shape["tp"] == 2
    return jax.shard_map(
        fused if one_kernel else plain,
        mesh=mesh,
        in_specs=(
            P("ep", "tp"),
            P("ep", None),
            P("ep", None),
            P("ep", None, "tp"),
            P("ep", None, "tp"),
            P("ep", None, "tp"),
        ),
        out_specs=P("ep", "tp"),
        check_vma=False,
    )
```

```python
import functools

import jax
import jax.numpy as jnp
from jax import lax
from jax.experimental import pallas as pl
from jax.experimental.pallas import tpu as pltpu
from jax.sharding import PartitionSpec as P

MESH = pl.DeviceIdType.MESH
LANES = 128


def share_of(expert_ids, gate_weights, n_experts):
    experts = jnp.arange(n_experts, dtype=jnp.int32)
    chosen = expert_ids[:, :, None] == experts[None, None, :]
    return jnp.sum(jnp.where(chosen, gate_weights[:, :, None], 0.0), axis=1)


def plain(tokens, expert_ids, gate_weights, w_gate, w_up, w_down):
    n_experts = lax.axis_size("ep")
    share = share_of(expert_ids, gate_weights, n_experts)
    share = lax.all_gather(share, "ep", axis=0, tiled=True)
    mine = jnp.arange(n_experts, dtype=jnp.int32) == lax.axis_index("ep")
    share = jnp.sum(jnp.where(mine[None, :], share, 0.0), axis=1, keepdims=True)
    rows = lax.all_gather(tokens, "tp", axis=1, tiled=True)
    rows = lax.all_gather(rows, "ep", axis=0, tiled=True)
    gate_sum = jnp.dot(rows, w_gate[0], preferred_element_type=jnp.float32)
    up_sum = jnp.dot(rows, w_up[0], preferred_element_type=jnp.float32)
    hidden = (jax.nn.silu(gate_sum) * up_sum).astype(jnp.bfloat16)
    hidden = lax.all_gather(hidden, "tp", axis=1, tiled=True)
    result = jnp.dot(hidden, w_down[0], preferred_element_type=jnp.float32)
    result = (result * share).astype(jnp.bfloat16)
    return lax.psum_scatter(result, "ep", scatter_dimension=0, tiled=True)


def kernel(tok, shares, wg_hbm, wu_hbm, wd_hbm, out,
           x_buf, wg, wu, wd, hid, acc, part, r0, s0, r1, s1, r2, sh, col,
           w_sem, own_sem, own_s, own_r, sh_s, sh_r, zu_s, zu_r, zd_s, zd_r, s_s, s_r, t_s, t_r, b_s, b_r,
           h_s, h_r, q0_s, q0_r, q1_s, q1_r, q2_s, q2_r):
    e = lax.axis_index("ep")
    y = lax.axis_index("tp")
    z, x, c = e // 4, (e // 2) % 2, e % 2
    zh, zl = z // 2, z % 2
    wide = tok.shape[1] // 2
    n_q = part.shape[0]
    q_cols = part.shape[3]

    def at(z_, x_, c_, y_):
        return ((z_ * 2 + x_) * 2 + c_, y_)

    z_of = [z, zh * 2 + 1 - zl, (1 - zh) * 2 + zl, (1 - zh) * 2 + 1 - zl]
    sib = at(z, x, 1 - c, y)
    x_peer = at(z, 1 - x, c, y)
    y_peer = (e, 1 - y)
    sx, sy = x + (1 - c) * (1 - 2 * x), y + c * (1 - 2 * y)
    tx, ty = x + c * (1 - 2 * x), y + (1 - c) * (1 - 2 * y)
    s_peer, t_peer = at(z, sx, c, sy), at(z, tx, c, ty)

    def block(z_, x_, y_, c_):
        return x_buf.at[2 * y_ + c_, :, pl.ds(16 * (4 * x_ + z_), 16), :]

    def own_block(color, c_):
        return x_buf.at[2 * y + color, c_, pl.ds(16 * (4 * x + z), 16), :]

    def remote(src, dst, ss, rs, dev):
        return pltpu.make_async_remote_copy(
            src_ref=src, dst_ref=dst, send_sem=ss, recv_sem=rs, device_id=dev, device_id_type=MESH
        )

    loads = []
    for k in range(4):
        kb = pl.ds(k * wide, wide)
        loads.append(pltpu.make_async_copy(wg_hbm.at[0, kb, :], wg.at[k], w_sem.at[2 * k]))
        loads.append(pltpu.make_async_copy(wu_hbm.at[0, kb, :], wu.at[k], w_sem.at[2 * k + 1]))
    half = wd.shape[1]
    for k in range(2):
        loads.append(
            pltpu.make_async_copy(wd_hbm.at[0, pl.ds(k * half, half), :], wd.at[k], w_sem.at[8 + k])
        )

    barrier = pltpu.get_barrier_semaphore()
    for i in range(1, 16):
        pl.semaphore_signal(barrier, inc=1, device_id=((e + i) % 16, y), device_id_type=MESH)
    pl.semaphore_signal(barrier, inc=1, device_id=y_peer, device_id_type=MESH)
    own = [
        pltpu.make_async_copy(tok.at[:, pl.ds(k * wide, wide)], own_block(k, c), own_sem.at[k])
        for k in range(2)
    ]
    for cp in own:
        cp.start()
    pl.semaphore_wait(barrier, 16)

    sent = []

    def go(src, dst, ss, rs, dev):
        cp = remote(src, dst, ss, rs, dev)
        cp.start()
        sent.append(cp)

    for k in range(2):
        go(tok.at[:, pl.ds(k * wide, wide)], own_block(k, c), own_s.at[k], own_r.at[k], sib)

    own[0].wait()
    own[1].wait()
    for k in range(2):
        remote(own_block(k, 1 - c), own_block(k, 1 - c), own_s.at[k], own_r.at[k], sib).wait_recv()

    def same(ref, ss, rs, dev):
        go(ref, ref, ss, rs, dev)

    def got(ref, rs):
        remote(ref, ref, own_s.at[0], rs, sib).wait_recv()

    mine = block(z, x, y, c)

    def up(d):
        b = block(z - d + 1, x, y, c)
        return remote(b, b, zu_s.at[d - 1], zu_r.at[d - 1], at(z + 1, x, c, y))

    def down(d):
        b = block(z + d - 1, x, y, c)
        return remote(b, b, zd_s.at[d - 1], zd_r.at[d - 1], at(z - 1, x, c, y))

    def up_goes(d):
        return (z < 3) & (z >= d - 1)

    def down_goes(d):
        return (z > 0) & (z <= 4 - d)

    def pair(ref, ss, rs, i, dev):
        return remote(ref, ref, ss.at[i], rs.at[i], dev)

    pl.when(up_goes(1))(lambda: up(1).start())
    pl.when(down_goes(1))(lambda: down(1).start())
    pair(mine, t_s, t_r, z, t_peer).start()
    pair(mine, s_s, s_r, z, s_peer).start()

    pos = (c * 2 + x) * 4 + z
    for i in range(1, 16):
        to = (e + i) % 16
        go(shares.at[to], sh.at[pos], sh_s.at[i - 1], sh_r.at[i - 1], (to, y))
    own_share = pltpu.make_async_copy(shares.at[e], sh.at[pos], own_sem.at[2])
    own_share.start()
    for cp in loads:
        cp.start()

    def landed(zp, moving, d, coming):
        b = block(zp, x, y, c)
        got(b, coming.at[d - 1])
        if d < 3:
            goes = up_goes(d + 1) if moving == "up" else down_goes(d + 1)
            pl.when(goes)(lambda: (up if moving == "up" else down)(d + 1).start())
        pair(b, s_s, s_r, zp, s_peer).start()
        pair(b, t_s, t_r, zp, t_peer).start()
        pair(b, b_s, b_r, zp, sib).start()

    def landed_s(zp):
        b = block(zp, sx, sy, c)
        got(b, s_r.at[zp])
        pair(b, t_s, t_r, 4 + zp, t_peer).start()
        pair(b, b_s, b_r, 4 + zp, sib).start()

    def landed_t(zp):
        b = block(zp, tx, ty, c)
        got(b, t_r.at[zp])
        pair(b, b_s, b_r, 8 + zp, sib).start()

    for d in range(1, 4):
        pl.when(z >= d)(lambda d=d: landed(z - d, "up", d, zu_r))
        pl.when(z + d <= 3)(lambda d=d: landed(z + d, "down", d, zd_r))
        if d == 1:
            landed_s(z)
            landed_t(z)
        else:
            for f in (landed_s, landed_t):
                pl.when(z >= d - 1)(lambda d=d, f=f: f(z - d + 1))
                pl.when(z + d - 1 <= 3)(lambda d=d, f=f: f(z + d - 1))
    for f in (landed_s, landed_t):
        pl.when(z >= 3)(lambda f=f: f(z - 3))
        pl.when(z <= 0)(lambda f=f: f(z + 3))
    for d in range(4):
        def landed_ts(zp):
            b = block(zp, 1 - x, 1 - y, c)
            got(b, t_r.at[4 + zp])
            pair(b, b_s, b_r, 12 + zp, sib).start()
        pl.when(z >= d)(lambda d=d, f=landed_ts: f(z - d))
        if d:
            pl.when(z + d <= 3)(lambda d=d, f=landed_ts: f(z + d))

    own_share.wait()
    for i in range(1, 16):
        remote(sh.at[pos], sh.at[pos], sh_s.at[i - 1], sh_r.at[i - 1], sib).wait_recv()
    pick = lax.broadcasted_iota(jnp.int32, (16, LANES), 0) == lax.broadcasted_iota(
        jnp.int32, (16, LANES), 1
    )
    for p in range(16):
        row = jnp.where(pick, sh[p], 0.0)
        col[pl.ds(16 * p, 16), :] = jnp.sum(row, axis=1, keepdims=True)

    for d in range(1, 4):
        got(mine, b_r.at[z_of[d]])
    for i in range(4, 16):
        got(mine, b_r.at[i])
    for cp in loads[:8]:
        cp.wait()

    rows = 256
    n_h = h_s.shape[0]
    h_cols = hid.shape[2] // n_h

    def hidden_copy(n):
        ref = hid.at[y, :, pl.ds(pl.multiple_of(n * h_cols, h_cols), h_cols)]
        return remote(ref, ref, h_s.at[n], h_r.at[n], y_peer)

    @pl.loop(0, n_h)
    def _(n):
        cols = pl.ds(pl.multiple_of(n * h_cols, h_cols), h_cols)
        g = jnp.zeros((rows, h_cols), jnp.float32)
        u = jnp.zeros((rows, h_cols), jnp.float32)
        for k in range(4):
            xk = x_buf[k].reshape(rows, wide)
            g = g + jnp.dot(xk, wg[k, :, cols], preferred_element_type=jnp.float32)
            u = u + jnp.dot(xk, wu[k, :, cols], preferred_element_type=jnp.float32)
        hid[y, :, cols] = (g / (1.0 + jnp.exp(-g)) * u).astype(jnp.bfloat16)
        hidden_copy(n).start()

    for cp in loads[8:]:
        cp.wait()

    @pl.loop(0, n_q)
    def _(q):
        cols = pl.ds(pl.multiple_of(q * q_cols, q_cols), q_cols)
        acc[:, cols] = jnp.dot(hid[y], wd[y, :, cols], preferred_element_type=jnp.float32)

    for n in range(n_h):
        hidden_copy(n).wait()

    def r0_copy(q):
        return remote(part.at[q, 1 - c], r0.at[q], q0_s.at[q], q0_r.at[q], sib)

    def r1_copy(q):
        src = s0.at[q, pl.ds(64 * (1 - x), 64), :]
        return remote(src, r1.at[q], q1_s.at[q], q1_r.at[q], x_peer)

    def r2_copy(q, k):
        src = s1.at[q, pl.ds(16 * z_of[k], 16), :]
        return remote(
            src, r2.at[q, k - 1], q2_s.at[3 * q + k - 1], q2_r.at[3 * q + k - 1], at(z_of[k], x, c, y)
        )

    f32 = jnp.float32

    @pl.loop(0, n_q + 5)
    def _(i):
        @pl.when(i < n_q)
        def _():
            cols = pl.ds(pl.multiple_of(i * q_cols, q_cols), q_cols)
            r = acc[:, cols] + jnp.dot(hid[1 - y], wd[1 - y, :, cols], preferred_element_type=f32)
            part[i] = (r * col[...]).astype(jnp.bfloat16).reshape(2, rows // 2, q_cols)
            r0_copy(i).start()

        @pl.when((i >= 1) & (i < n_q + 1))
        def _():
            q = i - 1
            r0_copy(q).wait()
            s0[q] = (part[q, c].astype(f32) + r0[q].astype(f32)).astype(jnp.bfloat16)
            r1_copy(q).start()

        @pl.when((i >= 3) & (i < n_q + 3))
        def _():
            q = i - 3
            r1_copy(q).wait()
            keep = s0[q, pl.ds(pl.multiple_of(64 * x, 64), 64), :].astype(f32)
            s1[q] = (keep + r1[q].astype(f32)).astype(jnp.bfloat16)
            for k in range(1, 4):
                r2_copy(q, k).start()

        @pl.when(i >= 5)
        def _():
            q = i - 5
            total = s1[q, pl.ds(pl.multiple_of(16 * z, 16), 16), :].astype(f32)
            for k in range(1, 4):
                r2_copy(q, k).wait()
                total = total + r2[q, k - 1].astype(f32)
            out[:, pl.ds(pl.multiple_of(q * q_cols, q_cols), q_cols)] = total.astype(jnp.bfloat16)

    for d in range(1, 4):
        pl.when(up_goes(d))(lambda d=d: up(d).wait_send())
        pl.when(down_goes(d))(lambda d=d: down(d).wait_send())
        pair(mine, b_s, b_r, z_of[d], sib).wait_send()
    for i in range(4):
        pair(mine, s_s, s_r, i, s_peer).wait_send()
    for i in range(8):
        pair(mine, t_s, t_r, i, t_peer).wait_send()
    for i in range(4, 16):
        pair(mine, b_s, b_r, i, sib).wait_send()
    for cp in sent:
        cp.wait_send()


def fused(tokens, expert_ids, gate_weights, w_gate, w_up, w_down):
    bf16, f32 = jnp.bfloat16, jnp.float32
    width = tokens.shape[1]
    depth, units = w_gate.shape[1], w_gate.shape[2]
    share = share_of(expert_ids, gate_weights, 16).T
    share = jnp.pad(share, ((0, 0), (0, LANES - 16)))[:, None, :]
    n_q, n_h = 7, 4
    q_cols = width // n_q
    wide = width // 2
    vmem, dma = pltpu.VMEM, pltpu.SemaphoreType.DMA
    hbm = pl.BlockSpec(memory_space=pl.ANY)
    return pl.pallas_call(
        kernel,
        out_shape=jax.ShapeDtypeStruct((16, width), bf16),
        in_specs=[hbm] * 5,
        out_specs=pl.BlockSpec(memory_space=pltpu.VMEM),
        scratch_shapes=[
            vmem((4, 2, 128, wide), bf16),
            vmem((4, wide, units), bf16),
            vmem((4, wide, units), bf16),
            vmem((2, units, width), bf16),
            vmem((2, 256, units), bf16),
            vmem((256, width), f32),
            vmem((n_q, 2, 128, q_cols), bf16),
            vmem((n_q, 128, q_cols), bf16),
            vmem((n_q, 128, q_cols), bf16),
            vmem((n_q, 64, q_cols), bf16),
            vmem((n_q, 64, q_cols), bf16),
            vmem((n_q, 3, 16, q_cols), bf16),
            vmem((16, 1, LANES), f32),
            vmem((256, 1), f32),
            dma((10,)), dma((3,)), dma((2,)), dma((2,)), dma((15,)), dma((15,)),
            dma((3,)), dma((3,)), dma((3,)), dma((3,)), dma((4,)), dma((4,)), dma((8,)), dma((8,)),
            dma((16,)), dma((16,)),
            dma((n_h,)), dma((n_h,)),
            dma((n_q,)), dma((n_q,)), dma((n_q,)), dma((n_q,)), dma((3 * n_q,)), dma((3 * n_q,)),
        ],
        compiler_params=pltpu.CompilerParams(
            collective_id=0, has_side_effects=True, vmem_limit_bytes=62_000_000
        ),
        cost_estimate=pl.CostEstimate(
            flops=2 * 256 * (depth * units * 2 + 2 * units * width),
            bytes_accessed=2 * (2 * depth * units + 2 * units * width),
            transcendentals=256 * units,
        ),
    )(tokens, share, w_gate, w_up, w_down)


def solution(mesh):
    one_kernel = mesh.shape["ep"] == 16 and mesh.shape["tp"] == 2
    return jax.shard_map(
        fused if one_kernel else plain,
        mesh=mesh,
        in_specs=(
            P("ep", "tp"),
            P("ep", None),
            P("ep", None),
            P("ep", None, "tp"),
            P("ep", None, "tp"),
            P("ep", None, "tp"),
        ),
        out_specs=P("ep", "tp"),
        check_vma=False,
    )
```

```python
import functools

import jax
import jax.numpy as jnp
from jax import lax
from jax.experimental import pallas as pl
from jax.experimental.pallas import tpu as pltpu
from jax.sharding import PartitionSpec as P

MESH = pl.DeviceIdType.MESH
LANES = 128


def share_of(expert_ids, gate_weights, n_experts):
    experts = jnp.arange(n_experts, dtype=jnp.int32)
    chosen = expert_ids[:, :, None] == experts[None, None, :]
    return jnp.sum(jnp.where(chosen, gate_weights[:, :, None], 0.0), axis=1)


def plain(tokens, expert_ids, gate_weights, w_gate, w_up, w_down):
    n_experts = lax.axis_size("ep")
    share = share_of(expert_ids, gate_weights, n_experts)
    share = lax.all_gather(share, "ep", axis=0, tiled=True)
    mine = jnp.arange(n_experts, dtype=jnp.int32) == lax.axis_index("ep")
    share = jnp.sum(jnp.where(mine[None, :], share, 0.0), axis=1, keepdims=True)
    rows = lax.all_gather(tokens, "tp", axis=1, tiled=True)
    rows = lax.all_gather(rows, "ep", axis=0, tiled=True)
    gate_sum = jnp.dot(rows, w_gate[0], preferred_element_type=jnp.float32)
    up_sum = jnp.dot(rows, w_up[0], preferred_element_type=jnp.float32)
    hidden = (jax.nn.silu(gate_sum) * up_sum).astype(jnp.bfloat16)
    hidden = lax.all_gather(hidden, "tp", axis=1, tiled=True)
    result = jnp.dot(hidden, w_down[0], preferred_element_type=jnp.float32)
    result = (result * share).astype(jnp.bfloat16)
    return lax.psum_scatter(result, "ep", scatter_dimension=0, tiled=True)


def kernel(tok, shares, wg_hbm, wu_hbm, wd_hbm, out,
           x_buf, wg, wu, wd, hid, acc, part, r0, s0, r1, s1, r2, sh, col,
           w_sem, own_sem, own_s, own_r, sh_s, sh_r, zu_s, zu_r, zd_s, zd_r, s_s, s_r, t_s, t_r, b_s, b_r,
           h_s, h_r, q0_s, q0_r, q1_s, q1_r, q2_s, q2_r):
    e = lax.axis_index("ep")
    y = lax.axis_index("tp")
    z, x, c = e // 4, (e // 2) % 2, e % 2
    zh, zl = z // 2, z % 2
    wide = tok.shape[1] // 2
    n_q = part.shape[0]
    q_cols = part.shape[3]

    def at(z_, x_, c_, y_):
        return ((z_ * 2 + x_) * 2 + c_, y_)

    z_of = [z, zh * 2 + 1 - zl, (1 - zh) * 2 + zl, (1 - zh) * 2 + 1 - zl]
    sib = at(z, x, 1 - c, y)
    x_peer = at(z, 1 - x, c, y)
    y_peer = (e, 1 - y)
    sx, sy = x + (1 - c) * (1 - 2 * x), y + c * (1 - 2 * y)
    tx, ty = x + c * (1 - 2 * x), y + (1 - c) * (1 - 2 * y)
    s_peer, t_peer = at(z, sx, c, sy), at(z, tx, c, ty)

    def block(z_, x_, y_, c_):
        return x_buf.at[2 * y_ + c_, :, pl.ds(16 * (4 * x_ + z_), 16), :]

    def own_block(color, c_):
        return x_buf.at[2 * y + color, c_, pl.ds(16 * (4 * x + z), 16), :]

    def remote(src, dst, ss, rs, dev):
        return pltpu.make_async_remote_copy(
            src_ref=src, dst_ref=dst, send_sem=ss, recv_sem=rs, device_id=dev, device_id_type=MESH
        )

    loads = []
    for k in range(4):
        kb = pl.ds(k * wide, wide)
        loads.append(pltpu.make_async_copy(wg_hbm.at[0, kb, :], wg.at[k], w_sem.at[2 * k]))
        loads.append(pltpu.make_async_copy(wu_hbm.at[0, kb, :], wu.at[k], w_sem.at[2 * k + 1]))
    half = wd.shape[1]
    for k in range(2):
        loads.append(
            pltpu.make_async_copy(wd_hbm.at[0, pl.ds(k * half, half), :], wd.at[k], w_sem.at[8 + k])
        )

    barrier = pltpu.get_barrier_semaphore()
    for i in range(1, 16):
        pl.semaphore_signal(barrier, inc=1, device_id=((e + i) % 16, y), device_id_type=MESH)
    pl.semaphore_signal(barrier, inc=1, device_id=y_peer, device_id_type=MESH)
    own = [
        pltpu.make_async_copy(tok.at[:, pl.ds(k * wide, wide)], own_block(k, c), own_sem.at[k])
        for k in range(2)
    ]
    for cp in own:
        cp.start()
    pl.semaphore_wait(barrier, 16)

    sent = []

    def go(src, dst, ss, rs, dev):
        cp = remote(src, dst, ss, rs, dev)
        cp.start()
        sent.append(cp)

    for k in range(2):
        go(tok.at[:, pl.ds(k * wide, wide)], own_block(k, c), own_s.at[k], own_r.at[k], sib)

    own[0].wait()
    own[1].wait()
    for k in range(2):
        remote(own_block(k, 1 - c), own_block(k, 1 - c), own_s.at[k], own_r.at[k], sib).wait_recv()

    def same(ref, ss, rs, dev):
        go(ref, ref, ss, rs, dev)

    def got(ref, rs):
        remote(ref, ref, own_s.at[0], rs, sib).wait_recv()

    mine = block(z, x, y, c)

    def up(d):
        b = block(z - d + 1, x, y, c)
        return remote(b, b, zu_s.at[d - 1], zu_r.at[d - 1], at(z + 1, x, c, y))

    def down(d):
        b = block(z + d - 1, x, y, c)
        return remote(b, b, zd_s.at[d - 1], zd_r.at[d - 1], at(z - 1, x, c, y))

    def up_goes(d):
        return (z < 3) & (z >= d - 1)

    def down_goes(d):
        return (z > 0) & (z <= 4 - d)

    def pair(ref, ss, rs, i, dev):
        return remote(ref, ref, ss.at[i], rs.at[i], dev)

    pl.when(up_goes(1))(lambda: up(1).start())
    pl.when(down_goes(1))(lambda: down(1).start())
    pair(mine, t_s, t_r, z, t_peer).start()
    pair(mine, s_s, s_r, z, s_peer).start()

    pos = (c * 2 + x) * 4 + z
    for i in range(1, 16):
        to = (e + i) % 16
        go(shares.at[to], sh.at[pos], sh_s.at[i - 1], sh_r.at[i - 1], (to, y))
    own_share = pltpu.make_async_copy(shares.at[e], sh.at[pos], own_sem.at[2])
    own_share.start()
    for cp in loads:
        cp.start()

    def landed(zp, moving, d, coming):
        b = block(zp, x, y, c)
        got(b, coming.at[d - 1])
        if d < 3:
            goes = up_goes(d + 1) if moving == "up" else down_goes(d + 1)
            pl.when(goes)(lambda: (up if moving == "up" else down)(d + 1).start())
        pair(b, s_s, s_r, zp, s_peer).start()
        pair(b, t_s, t_r, zp, t_peer).start()
        pair(b, b_s, b_r, zp, sib).start()

    def landed_s(zp):
        b = block(zp, sx, sy, c)
        got(b, s_r.at[zp])
        pair(b, t_s, t_r, 4 + zp, t_peer).start()
        pair(b, b_s, b_r, 4 + zp, sib).start()

    def landed_t(zp):
        b = block(zp, tx, ty, c)
        got(b, t_r.at[zp])
        pair(b, b_s, b_r, 8 + zp, sib).start()

    for d in range(1, 4):
        pl.when(z >= d)(lambda d=d: landed(z - d, "up", d, zu_r))
        pl.when(z + d <= 3)(lambda d=d: landed(z + d, "down", d, zd_r))
        if d == 1:
            landed_s(z)
            landed_t(z)
        else:
            for f in (landed_s, landed_t):
                pl.when(z >= d - 1)(lambda d=d, f=f: f(z - d + 1))
                pl.when(z + d - 1 <= 3)(lambda d=d, f=f: f(z + d - 1))
    for f in (landed_s, landed_t):
        pl.when(z >= 3)(lambda f=f: f(z - 3))
        pl.when(z <= 0)(lambda f=f: f(z + 3))
    for d in range(4):
        def landed_ts(zp):
            b = block(zp, 1 - x, 1 - y, c)
            got(b, t_r.at[4 + zp])
            pair(b, b_s, b_r, 12 + zp, sib).start()
        pl.when(z >= d)(lambda d=d, f=landed_ts: f(z - d))
        if d:
            pl.when(z + d <= 3)(lambda d=d, f=landed_ts: f(z + d))

    own_share.wait()
    for i in range(1, 16):
        remote(sh.at[pos], sh.at[pos], sh_s.at[i - 1], sh_r.at[i - 1], sib).wait_recv()
    pick = lax.broadcasted_iota(jnp.int32, (16, LANES), 0) == lax.broadcasted_iota(
        jnp.int32, (16, LANES), 1
    )
    for p in range(16):
        row = jnp.where(pick, sh[p], 0.0)
        col[pl.ds(16 * p, 16), :] = jnp.sum(row, axis=1, keepdims=True)

    for d in range(1, 4):
        got(mine, b_r.at[z_of[d]])
    for i in range(4, 16):
        got(mine, b_r.at[i])
    for cp in loads[:8]:
        cp.wait()

    rows = 256
    n_h = h_s.shape[0]
    h_cols = hid.shape[2] // n_h

    def hidden_copy(n):
        ref = hid.at[y, :, pl.ds(pl.multiple_of(n * h_cols, h_cols), h_cols)]
        return remote(ref, ref, h_s.at[n], h_r.at[n], y_peer)

    @pl.loop(0, n_h)
    def _(n):
        cols = pl.ds(pl.multiple_of(n * h_cols, h_cols), h_cols)
        g = jnp.zeros((rows, h_cols), jnp.float32)
        u = jnp.zeros((rows, h_cols), jnp.float32)
        for k in range(4):
            xk = x_buf[k].reshape(rows, wide)
            g = g + jnp.dot(xk, wg[k, :, cols], preferred_element_type=jnp.float32)
            u = u + jnp.dot(xk, wu[k, :, cols], preferred_element_type=jnp.float32)
        hid[y, :, cols] = (g / (1.0 + jnp.exp(-g)) * u).astype(jnp.bfloat16)
        hidden_copy(n).start()

    for cp in loads[8:]:
        cp.wait()

    @pl.loop(0, n_q)
    def _(q):
        cols = pl.ds(pl.multiple_of(q * q_cols, q_cols), q_cols)
        acc[:, cols] = jnp.dot(hid[y], wd[y, :, cols], preferred_element_type=jnp.float32)

    for n in range(n_h):
        hidden_copy(n).wait()

    def r0_copy(q):
        return remote(part.at[q, 1 - c], r0.at[q], q0_s.at[q], q0_r.at[q], sib)

    def r1_copy(q):
        src = s0.at[q, pl.ds(64 * (1 - x), 64), :]
        return remote(src, r1.at[q], q1_s.at[q], q1_r.at[q], x_peer)

    def r2_copy(q, k):
        src = s1.at[q, pl.ds(16 * z_of[k], 16), :]
        return remote(
            src, r2.at[q, k - 1], q2_s.at[3 * q + k - 1], q2_r.at[3 * q + k - 1], at(z_of[k], x, c, y)
        )

    f32 = jnp.float32

    @pl.loop(0, n_q + 7)
    def _(i):
        @pl.when(i < n_q)
        def _():
            cols = pl.ds(pl.multiple_of(i * q_cols, q_cols), q_cols)
            r = acc[:, cols] + jnp.dot(hid[1 - y], wd[1 - y, :, cols], preferred_element_type=f32)
            part[i] = (r * col[...]).astype(jnp.bfloat16).reshape(2, rows // 2, q_cols)
            r0_copy(i).start()

        @pl.when((i >= 1) & (i < n_q + 1))
        def _():
            q = i - 1
            r0_copy(q).wait()
            s0[q] = (part[q, c].astype(f32) + r0[q].astype(f32)).astype(jnp.bfloat16)
            r1_copy(q).start()

        @pl.when((i >= 4) & (i < n_q + 4))
        def _():
            q = i - 4
            r1_copy(q).wait()
            keep = s0[q, pl.ds(pl.multiple_of(64 * x, 64), 64), :].astype(f32)
            s1[q] = (keep + r1[q].astype(f32)).astype(jnp.bfloat16)
            for k in range(1, 4):
                r2_copy(q, k).start()

        @pl.when(i >= 7)
        def _():
            q = i - 7
            total = s1[q, pl.ds(pl.multiple_of(16 * z, 16), 16), :].astype(f32)
            for k in range(1, 4):
                r2_copy(q, k).wait()
                total = total + r2[q, k - 1].astype(f32)
            out[:, pl.ds(pl.multiple_of(q * q_cols, q_cols), q_cols)] = total.astype(jnp.bfloat16)

    for d in range(1, 4):
        pl.when(up_goes(d))(lambda d=d: up(d).wait_send())
        pl.when(down_goes(d))(lambda d=d: down(d).wait_send())
        pair(mine, b_s, b_r, z_of[d], sib).wait_send()
    for i in range(4):
        pair(mine, s_s, s_r, i, s_peer).wait_send()
    for i in range(8):
        pair(mine, t_s, t_r, i, t_peer).wait_send()
    for i in range(4, 16):
        pair(mine, b_s, b_r, i, sib).wait_send()
    for cp in sent:
        cp.wait_send()


def fused(tokens, expert_ids, gate_weights, w_gate, w_up, w_down):
    bf16, f32 = jnp.bfloat16, jnp.float32
    width = tokens.shape[1]
    depth, units = w_gate.shape[1], w_gate.shape[2]
    share = share_of(expert_ids, gate_weights, 16).T
    share = jnp.pad(share, ((0, 0), (0, LANES - 16)))[:, None, :]
    n_q, n_h = 7, 4
    q_cols = width // n_q
    wide = width // 2
    vmem, dma = pltpu.VMEM, pltpu.SemaphoreType.DMA
    hbm = pl.BlockSpec(memory_space=pl.ANY)
    return pl.pallas_call(
        kernel,
        out_shape=jax.ShapeDtypeStruct((16, width), bf16),
        in_specs=[hbm] * 5,
        out_specs=pl.BlockSpec(memory_space=pltpu.VMEM),
        scratch_shapes=[
            vmem((4, 2, 128, wide), bf16),
            vmem((4, wide, units), bf16),
            vmem((4, wide, units), bf16),
            vmem((2, units, width), bf16),
            vmem((2, 256, units), bf16),
            vmem((256, width), f32),
            vmem((n_q, 2, 128, q_cols), bf16),
            vmem((n_q, 128, q_cols), bf16),
            vmem((n_q, 128, q_cols), bf16),
            vmem((n_q, 64, q_cols), bf16),
            vmem((n_q, 64, q_cols), bf16),
            vmem((n_q, 3, 16, q_cols), bf16),
            vmem((16, 1, LANES), f32),
            vmem((256, 1), f32),
            dma((10,)), dma((3,)), dma((2,)), dma((2,)), dma((15,)), dma((15,)),
            dma((3,)), dma((3,)), dma((3,)), dma((3,)), dma((4,)), dma((4,)), dma((8,)), dma((8,)),
            dma((16,)), dma((16,)),
            dma((n_h,)), dma((n_h,)),
            dma((n_q,)), dma((n_q,)), dma((n_q,)), dma((n_q,)), dma((3 * n_q,)), dma((3 * n_q,)),
        ],
        compiler_params=pltpu.CompilerParams(
            collective_id=0, has_side_effects=True, vmem_limit_bytes=62_000_000
        ),
        cost_estimate=pl.CostEstimate(
            flops=2 * 256 * (depth * units * 2 + 2 * units * width),
            bytes_accessed=2 * (2 * depth * units + 2 * units * width),
            transcendentals=256 * units,
        ),
    )(tokens, share, w_gate, w_up, w_down)


def solution(mesh):
    one_kernel = mesh.shape["ep"] == 16 and mesh.shape["tp"] == 2
    return jax.shard_map(
        fused if one_kernel else plain,
        mesh=mesh,
        in_specs=(
            P("ep", "tp"),
            P("ep", None),
            P("ep", None),
            P("ep", None, "tp"),
            P("ep", None, "tp"),
            P("ep", None, "tp"),
        ),
        out_specs=P("ep", "tp"),
        check_vma=False,
    )
```
